32 devices in a mesh: mesh: 8 (over z, core), band: 4 (over y, x).
Axes of the slice: x: 2, y: 2, z: 4, core: 2. Of those that a mesh axis runs over, the one named last changes fastest.
Arguments:
- filter_block: bfloat16 [512, 61440], P('band', 'mesh'), may hold values from -6 to 6
- local_pot: float32 [61440], P('mesh'), may hold values from 0.5 to 2
- cell_scale: float32 [1024], P('mesh'), may hold values from 0.5 to 2
- cell_kernel: bfloat16 [125, 125], replicated
- cell_map: int32 [125, 1024], P(None, 'mesh'), may hold values from 0 to 8191, as said below
- neighbour_ids: int32 [8, 6], P('mesh'), may hold values from 0 to 7, as said below
- send_nodes: int32 [8, 6, 64], P('mesh'), may hold values from 0 to 7679
- rotation_rows: bfloat16 [512, 512], P('band'), may hold values from -0.25 to 0.25
- panel_owner: int32 [2], replicated, may hold values from 0 to 3
Outputs:
- filtered: bfloat16 [512, 61440], P('band', 'mesh')
- rotated: bfloat16 [512, 61440], P(None, ('mesh', 'band'))
- state_energy: float32 [512], P('band')
The draws below stay inside these ranges and needn't reach their ends.
Inputs may be any that keep to these rules, and one draw needn't show every extreme that they name: `neighbour_ids`: row p lists 6 distinct partitions other than p; q is listed in row p exactly when p is listed in row q. `cell_map`: in the columns of partition p's cells an entry below 7680 names an owned node of p, and an entry 7680 + q*64 + g names slot g of a partition q listed in row p of neighbour_ids.
All inputs are finite; a program needn't handle non-finite values.
Results may differ from the reference program's by a relative error of at most 0.0059.
Values may be sent and summed in bfloat16 or wider, within the bound.
A program may use at most 64 MiB of HBM per device.

```python
import math
import jax
import jax.numpy as jnp
from jax import lax

STATES = 512
NPE = 125
GHOST = 64
PSTEPS = 2
CELLS_DEV = 128
STATE_DEV = 128
NBR = 6
NODE_DEV = 7680
EXT = 8192
NODES = 61440
CELLS = 1024
N_MESH = 8
N_BAND = 4


def neighbour_table(key):
    ordering = jax.random.permutation(jax.random.fold_in(key, 11), N_MESH).astype(jnp.int32)
    position = jnp.zeros((N_MESH,), jnp.int32).at[ordering].set(jnp.arange(N_MESH, dtype=jnp.int32))
    half_count = NBR // 2
    offsets = jnp.concatenate([jnp.arange(1, half_count + 1), -jnp.arange(1, half_count + 1)]).astype(jnp.int32)
    return ordering[(position[:, None] + offsets[None, :]) % N_MESH]


def draw_neighbour_ids(key, part):
    return neighbour_table(key)


def draw_cell_map(key, part):
    neighbours = neighbour_table(key)
    entry_count = NPE * CELLS_DEV
    covered = NBR * GHOST

    def one_part(part_id):
        part_key = jax.random.fold_in(jax.random.fold_in(key, 23), part_id)
        keys = jax.random.split(part_key, 5)
        entries = jnp.arange(entry_count, dtype=jnp.int32)
        own_random = jax.random.randint(keys[0], (entry_count,), 0, NODE_DEV, dtype=jnp.int32)
        is_ghost = jax.random.randint(keys[1], (entry_count,), 0, 3, dtype=jnp.int32) == 0
        chosen = jax.random.randint(keys[2], (entry_count,), 0, NBR, dtype=jnp.int32)
        slots = jax.random.randint(keys[3], (entry_count,), 0, GHOST, dtype=jnp.int32)
        row_list = neighbours[part_id]
        ghost_random = NODE_DEV + row_list[chosen] * GHOST + slots
        values_out = jnp.where(is_ghost, ghost_random, own_random)
        fixed_ghost = NODE_DEV + row_list[entries // GHOST % NBR] * GHOST + entries % GHOST
        fixed_own = (entries - covered) % NODE_DEV
        values_out = jnp.where(entries < covered, fixed_ghost, jnp.where(entries < covered + NODE_DEV, fixed_own, values_out))
        shuffle = jax.random.permutation(keys[4], entry_count)
        values_out = values_out[shuffle]
        return values_out.reshape(CELLS_DEV, NPE).T
    all_maps = lax.map(one_part, jnp.arange(N_MESH, dtype=jnp.int32))
    return all_maps.transpose(1, 0, 2).reshape(NPE, N_MESH * CELLS_DEV).astype(jnp.int32)


def draw_cell_kernel(key, part):
    keys = jax.random.split(key, 2)
    off_part = jax.random.normal(keys[0], (NPE, NPE), jnp.float32)
    off_part = off_part * (0.6 / jnp.sqrt(jnp.float32(NPE)))
    diagonal = jax.random.uniform(keys[1], (NPE,), jnp.float32, 1.5, 3.0)
    identity = jnp.eye(NPE, dtype=jnp.float32)
    return (off_part * (1.0 - identity) + identity * diagonal[:, None]).astype(jnp.bfloat16)


def with_ends(values, stream_key, smallest, high):
    index_at = [jax.random.randint(jax.random.fold_in(stream_key, axis), (), 0, length) for axis, length in enumerate(values.shape)]
    longest = values.shape.index(max(values.shape))
    next_to = index_at[:longest] + [(index_at[longest] + 1) % values.shape[longest]] + index_at[longest + 1:]
    return values.at[tuple(index_at)].set(smallest).at[tuple(next_to)].set(high)


def block_levels(key, dims, shards, least, top_value):
    def one(dim, shards_of):
        draws = jax.random.uniform(jax.random.fold_in(jax.random.fold_in(key, 6), dim), (shards_of,), jnp.float32, least / len(shards), top_value / len(shards))
        return jnp.repeat(jnp.exp(draws), dims[dim] // shards_of).reshape((-1,) + (1,) * (len(dims) - dim - 1))

    gain = one(*shards[0])
    for cut in shards[1:]:
        gain = gain * one(*cut)
    return gain


def bell_draw(stream_key, dims, width, most, shards=(), kind=jnp.bfloat16):
    values = jax.random.normal(stream_key, dims, jnp.float32) * width
    if len(shards) > 0:
        values = block_levels(stream_key, dims, shards, -0.22, 0.18) * values
    return jnp.clip(values, min=-most, max=most).astype(kind)


def setup_inputs(seed: int = 0) -> dict:
    key_of = jax.random.split(jax.random.key(seed), 10)
    return {
        "filter_block": bell_draw(key_of[0], (STATES, NODES), 1.0, 6.0, ((0, 4), (1, 8))),
        "local_pot": jnp.clip(0.5 + 1.5 * jax.random.uniform(key_of[1], (NODES,), jnp.float32) ** block_levels(key_of[1], (NODES,), ((0, 8),), -0.2, 0.2), 0.5, 2.0),
        "cell_scale": jnp.clip(jnp.exp(math.log(2.0) - 1.3862944 * jax.random.uniform(key_of[2], (CELLS,), jnp.float32) ** block_levels(key_of[2], (CELLS,), ((0, 8),), -0.2, 0.2)), 0.5, 2.0),
        "cell_kernel": draw_cell_kernel(jax.random.fold_in(key_of[9], 71), 0),
        "cell_map": draw_cell_map(jax.random.fold_in(key_of[9], 71), 0),
        "neighbour_ids": draw_neighbour_ids(jax.random.fold_in(key_of[9], 71), 0),
        "send_nodes": with_ends(jax.random.randint(key_of[6], (N_MESH, NBR, GHOST), 0, NODE_DEV), jax.random.fold_in(key_of[6], 1), 0, NODE_DEV - 1).astype(jnp.int32),
        "rotation_rows": bell_draw(key_of[7], (STATES, STATES), STATES ** -0.5, 0.25, ((0, 4),)),
        "panel_owner": jax.random.randint(key_of[8], (PSTEPS,), 0, N_BAND).astype(jnp.int32),
    }


center = 6.0
half_width = 4.0


def ghost_block(state_field, neighbour_ids, send_nodes, part_id):
    matches = neighbour_ids == part_id
    row_index = jnp.sum(jnp.where(matches[:, :, None], send_nodes, 0), axis=1).astype(jnp.int32)
    present = jnp.any(matches, axis=1)
    owners = jnp.arange(N_MESH, dtype=jnp.int32)[:, None]
    picked = state_field[:, owners, row_index]
    picked = jnp.where(present[None, :, None], picked, jnp.zeros_like(picked))
    return picked.reshape(STATES, N_MESH * GHOST)


def reference(filter_block, local_pot, cell_scale, cell_kernel, cell_map, neighbour_ids, send_nodes, rotation_rows, panel_owner):
    field_zero = filter_block.reshape(STATES, N_MESH, NODE_DEV)
    potential = local_pot.reshape(N_MESH, NODE_DEV)
    scales = cell_scale.reshape(N_MESH, CELLS_DEV)
    all_maps = cell_map.reshape(NPE, N_MESH, CELLS_DEV)
    kernel = cell_kernel.astype(jnp.float32)

    def operate(state_field, part_id):
        own_rows = state_field[:, part_id]
        ghosts = ghost_block(state_field, neighbour_ids, send_nodes, part_id)
        extended = jnp.concatenate([own_rows, ghosts], axis=1)
        cell_nodes = all_maps[:, part_id]
        gathered = jnp.take(extended, cell_nodes, axis=1).astype(jnp.float32)
        product = jnp.einsum("ab,sbc->sac", kernel, gathered) * scales[part_id]
        totals = jnp.zeros((STATES, EXT), jnp.float32).at[:, cell_nodes.reshape(-1)].add(product.reshape(STATES, -1))
        return totals[:, :NODE_DEV] + potential[part_id] * own_rows.astype(jnp.float32), own_rows

    def first_step(part_id):
        image_zero, own_rows = operate(field_zero, part_id)
        return ((image_zero - center * own_rows.astype(jnp.float32)) / half_width).astype(jnp.bfloat16)

    field_one = lax.map(first_step, jnp.arange(N_MESH, dtype=jnp.int32)).transpose(1, 0, 2)

    def second(part_id):
        image_one, own_rows = operate(field_one, part_id)
        own_float = own_rows.astype(jnp.float32)
        energy = jnp.sum(own_float * image_one, axis=1)
        start_field = field_zero[:, part_id].astype(jnp.float32)
        next_field = (2.0 * (image_one - center * own_float) / half_width - start_field).astype(jnp.bfloat16)
        return next_field, energy

    field_two, energies = lax.map(second, jnp.arange(N_MESH, dtype=jnp.int32))
    state_energy = jnp.sum(energies, axis=0) / NODES
    filtered = field_two.transpose(1, 0, 2).reshape(STATES, NODES)
    totals = jnp.zeros((STATES, NODES), jnp.float32)
    for step_id in range(PSTEPS):
        first_row = (panel_owner[step_id] * STATE_DEV).astype(jnp.int32)
        picked = lax.dynamic_slice_in_dim(filtered, first_row, STATE_DEV, 0).astype(jnp.float32)
        coefficients = lax.dynamic_slice_in_dim(rotation_rows, first_row, STATE_DEV, 0).astype(jnp.float32)
        totals = totals + jnp.dot(coefficients.T, picked, preferred_element_type=jnp.float32)
    return filtered, totals.astype(jnp.bfloat16), state_energy
```

```python
import functools

import jax
import jax.numpy as jnp
from jax import lax
from jax.experimental import pallas as pl
from jax.experimental.pallas import tpu as pltpu
from jax.sharding import PartitionSpec as P

center = 6.0
half_width = 4.0
LANES = 128
TABLES = 8
VMEM_BYTES = 56 * 1024 * 1024


def flat(ref):
    return ref.reshape(ref.shape[0], ref.shape[2])


def pack_rows(rows_ref, ids_ref, send_ref, packed_ref, out_ref):
    out_ref[...] = jnp.zeros_like(out_ref)
    slots = out_ref.shape[1]

    @pl.loop(0, ids_ref.shape[1])
    def _(r):
        for g in range(slots):
            packed_ref[g] = rows_ref[send_ref[r, g]]
        out_ref[ids_ref[0, r]] = flat(packed_ref)[...].astype(out_ref.dtype)


def apply_cells(map_ref, scale_ref, kernel_ref, pot_ref, own_ref, ghost_ref, ext, tables, gathers, products):
    nodes = own_ref.shape[0]
    npe, cells = map_ref.shape
    parts, slots, _ = ghost_ref.shape

    @pl.loop(0, nodes // LANES)
    def _(i):
        at = pl.ds(pl.multiple_of(i * LANES, LANES), LANES)
        block = own_ref[at, :]
        flat(ext)[at, :] = block.astype(jnp.float32)
        row = lax.broadcasted_iota(jnp.int32, (LANES, LANES), 0)
        column = lax.broadcasted_iota(jnp.int32, (LANES, LANES), 1)
        shifted = pot_ref[pl.ds(i, 1), :] - center
        diagonal = jnp.where(row == column, shifted, 0.0)
        high = diagonal.astype(jnp.bfloat16)
        low = (diagonal - high.astype(jnp.float32)).astype(jnp.bfloat16)
        flat(tables[0])[at, :] = jnp.dot(high, block, preferred_element_type=jnp.float32) + jnp.dot(
            low, block, preferred_element_type=jnp.float32
        )
        for table in tables[1:]:
            flat(table)[at, :] = jnp.zeros((LANES, table.shape[2]), jnp.float32)

    @pl.loop(0, parts)
    def _(q):
        start = pl.multiple_of(nodes + q * slots, slots)
        flat(ext)[pl.ds(start, slots), :] = ghost_ref[q].astype(jnp.float32)
        for table in tables:
            flat(table)[pl.ds(start, slots), :] = jnp.zeros((slots, table.shape[2]), jnp.float32)

    for ref in (*gathers, *products):
        ref[...] = jnp.zeros_like(ref)

    def stage(step, gather_out, gather_in, product_out, product_in):
        last = cells - 1
        take = jnp.minimum(step, last)
        middle = jnp.clip(step - 1, 0, last)
        put = jnp.clip(step - 2, 0, last)
        flat(product_out)[...] = (
            jnp.dot(kernel_ref[...], flat(gather_in)[...].astype(jnp.bfloat16), preferred_element_type=jnp.float32)
            * scale_ref[middle]
        )
        for first in range(0, npe, TABLES):
            group = range(first, min(first + TABLES, npe))
            rows = [ext[map_ref[b, take]] for b in group]
            where_to = [map_ref[a, put] for a in group]
            sums = [tables[a - first][at] + product_in[a] for a, at in zip(group, where_to)]
            for a, at, value in zip(group, where_to, sums):
                tables[a - first][at] = value
            for b, row in zip(group, rows):
                gather_out[b] = row

    @pl.loop(0, (cells + 3) // 2)
    def _(pair):
        stage(2 * pair, gathers[0], gathers[1], products[1], products[0])
        stage(2 * pair + 1, gathers[1], gathers[0], products[0], products[1])


def table_sum(tables, at):
    values = [flat(table)[at, :] for table in tables]
    while len(values) > 1:
        values = [a + b for a, b in zip(values[::2], values[1::2])]
    return values[0]


def first_kernel(
    map_ref, scale_ref, ids_ref, send_ref, kernel_ref, pot_ref, own_ref, ghost_ref,
    one_out, packed_out, ext, packed, *scratch,
):
    tables, gathers, products = scratch[:TABLES], scratch[TABLES : TABLES + 2], scratch[TABLES + 2 :]
    apply_cells(map_ref, scale_ref, kernel_ref, pot_ref, own_ref, ghost_ref, ext, tables, gathers, products)

    @pl.loop(0, own_ref.shape[0] // LANES)
    def _(i):
        at = pl.ds(pl.multiple_of(i * LANES, LANES), LANES)
        one = (table_sum(tables, at) * (1.0 / half_width)).astype(jnp.bfloat16)
        one_out[at, :] = one
        flat(ext)[at, :] = one.astype(jnp.float32)

    pack_rows(ext, ids_ref, send_ref, packed, packed_out)


def second_kernel(
    map_ref, scale_ref, kernel_ref, pot_ref, own_ref, ghost_ref, field_ref,
    filtered_out, pieces_out, energy_out, ext, *scratch,
):
    tables, gathers, products = scratch[:TABLES], scratch[TABLES : TABLES + 2], scratch[TABLES + 2 :]
    apply_cells(map_ref, scale_ref, kernel_ref, pot_ref, own_ref, ghost_ref, ext, tables, gathers, products)
    count = own_ref.shape[1]
    piece = pieces_out.shape[2] // LANES
    energy_out[...] = jnp.zeros_like(energy_out)

    @pl.loop(0, pieces_out.shape[0])
    def _(band):
        @pl.loop(0, piece)
        def _(j):
            here = pl.ds(pl.multiple_of(j * LANES, LANES), LANES)
            at = pl.ds(pl.multiple_of((band * piece + j) * LANES, LANES), LANES)
            total = table_sum(tables, at)
            one = flat(ext)[at, :]
            terms = one * (total + center * one)
            energy_out[...] += jnp.sum(terms.reshape(LANES // 8, 8, count), axis=0)
            turned = (total * (2.0 / half_width)).T
            value = (turned - field_ref[:, at].astype(jnp.float32)).astype(jnp.bfloat16)
            filtered_out[:, at] = value
            pieces_out[band, :, here] = value


def peer_at(axis, step):
    return lax.rem(lax.axis_index(axis) + step, lax.axis_size(axis))


def greet(axes):
    barrier = pltpu.get_barrier_semaphore()
    peers = 0
    for axis in axes:
        for step in range(1, lax.axis_size(axis)):
            pl.semaphore_signal(
                barrier, inc=1, device_id={axis: peer_at(axis, step)}, device_id_type=pl.DeviceIdType.MESH
            )
            peers += 1
    pl.semaphore_wait(barrier, peers)


def send(source, target, axis, step, send_sem, recv_sem):
    copy = pltpu.make_async_remote_copy(
        src_ref=source,
        dst_ref=target,
        send_sem=send_sem.at[step - 1],
        recv_sem=recv_sem.at[step - 1],
        device_id={axis: peer_at(axis, step)},
        device_id_type=pl.DeviceIdType.MESH,
    )
    copy.start()
    return copy


def turn_kernel(
    ids_ref, send_ref, field_ref, rotation_ref, rows_out, ghost_out, rotation_out,
    rows, packed, outgoing, send_sem, recv_sem, send_more, recv_more,
):
    nodes = field_ref.shape[1]
    parts, slots, _ = outgoing.shape
    band, me = lax.axis_index("band"), lax.axis_index("mesh")
    greet(("band", "mesh"))
    copies = [
        send(rotation_ref, rotation_out.at[band], "band", step, send_more, recv_more)
        for step in range(1, lax.axis_size("band"))
    ]
    rotation_out[band] = rotation_ref[...]

    @pl.loop(0, nodes // LANES)
    def _(i):
        at = pl.ds(pl.multiple_of(i * LANES, LANES), LANES)
        block = field_ref[:, at].astype(jnp.float32).T
        rows[at, :] = block
        rows_out[at, :] = block.astype(jnp.bfloat16)

    @pl.loop(0, parts)
    def _(q):
        place = jnp.int32(0)
        listed = jnp.int32(0)
        for r in range(ids_ref.shape[1]):
            same = ids_ref[0, r] == q
            place = jnp.where(same, r, place)
            listed = jnp.where(same, 1, listed)
        for g in range(slots):
            packed[g : g + 1, :] = rows[pl.ds(send_ref[place, g], 1), :]
        outgoing[q] = (packed[...] * listed.astype(jnp.float32)).astype(outgoing.dtype)

    copies += [
        send(outgoing.at[peer_at("mesh", step)], ghost_out.at[me], "mesh", step, send_sem, recv_sem)
        for step in range(1, lax.axis_size("mesh"))
    ]
    ghost_out[me] = jnp.zeros(ghost_out.shape[1:], ghost_out.dtype)
    for copy in copies:
        copy.wait()


def exchange_kernel(packed_ref, ghost_out, send_sem, recv_sem):
    me = lax.axis_index("mesh")
    greet(("mesh",))
    copies = [
        send(packed_ref.at[peer_at("mesh", step)], ghost_out.at[me], "mesh", step, send_sem, recv_sem)
        for step in range(1, lax.axis_size("mesh"))
    ]
    ghost_out[me] = jnp.zeros(ghost_out.shape[1:], ghost_out.dtype)
    for copy in copies:
        copy.wait()


def swap_kernel(pieces_ref, energy_ref, pieces_out, energy_out, keep_sem, send_sem, recv_sem, send_small, recv_small):
    band, me = lax.axis_index("band"), lax.axis_index("mesh")
    greet(("band", "mesh"))
    copies = [
        send(pieces_ref.at[peer_at("band", step)], pieces_out.at[band], "band", step, send_sem, recv_sem)
        for step in range(1, lax.axis_size("band"))
    ]
    copies += [
        send(energy_ref, energy_out.at[me], "mesh", step, send_small, recv_small)
        for step in range(1, lax.axis_size("mesh"))
    ]
    keep = pltpu.make_async_copy(pieces_ref.at[band], pieces_out.at[band], keep_sem)
    keep.start()
    energy_out[me] = energy_ref[...]
    for copy in copies:
        copy.wait()
    keep.wait()


def rotate_kernel(nodes_all, block, owner_ref, rotations, pieces_ref, energy_ref, out_ref, energy_out):
    steps = owner_ref.shape[0]
    rotation = jnp.concatenate([rotations[owner_ref[k]] for k in range(steps)], axis=0)
    turned = rotation.astype(jnp.float32).T.astype(jnp.bfloat16)
    parts = jnp.sum(energy_ref[...], axis=0)
    energy_out[...] = jnp.sum(parts, axis=0, keepdims=True) / nodes_all

    @pl.loop(0, pieces_ref.shape[2] // block)
    def _(j):
        at = pl.ds(pl.multiple_of(j * block, block), block)
        panel = jnp.concatenate([pieces_ref[owner_ref[k], :, at] for k in range(steps)], axis=0)
        out_ref[:, at] = jnp.dot(turned, panel, preferred_element_type=jnp.float32).astype(out_ref.dtype)


vmem = pl.BlockSpec(memory_space=pltpu.VMEM)
smem = pl.BlockSpec(memory_space=pltpu.SMEM)


anywhere = pl.BlockSpec(memory_space=pl.ANY)


def call(body, name, outs, in_specs, out_specs=None, scratch=(), traffic=None, collective=None):
    return pl.pallas_call(
        body,
        name=name,
        out_shape=outs,
        in_specs=in_specs,
        out_specs=out_specs or tuple(vmem for _ in outs),
        scratch_shapes=list(scratch),
        cost_estimate=traffic and pl.CostEstimate(flops=traffic, bytes_accessed=traffic, transcendentals=0),
        compiler_params=pltpu.CompilerParams(
            vmem_limit_bytes=VMEM_BYTES,
            collective_id=collective,
            has_side_effects=collective is not None,
        ),
    )


def per_device(
    filter_block, local_pot, cell_scale, cell_kernel, cell_map, neighbour_ids, send_nodes, rotation_rows, panel_owner
):
    count, nodes = filter_block.shape
    mesh_size, band_size = lax.axis_size("mesh"), lax.axis_size("band")
    slots = send_nodes.shape[2]
    extent = nodes + mesh_size * slots
    npe, cells = cell_map.shape
    side = -(-npe // LANES) * LANES
    lists = send_nodes[0]
    kernel = jnp.pad(cell_kernel, ((0, side - npe), (0, side - npe)))
    pot = local_pot.reshape(nodes // LANES, LANES)
    shape = jax.ShapeDtypeStruct
    f32, bf16 = jnp.float32, jnp.bfloat16
    width = nodes // band_size
    block = 3 * LANES if width % (3 * LANES) == 0 else LANES
    traffic = 5 * 4 * npe * cells * count

    def table(rows):
        return pltpu.VMEM((rows, 1, count), f32)

    rows = shape((nodes, count), bf16)
    packed = shape((mesh_size, slots, count), bf16)
    working = [table(extent) for _ in range(TABLES)] + [table(side) for _ in range(4)]
    dma = pltpu.SemaphoreType.DMA

    def exchange(outgoing, collective):
        sems = dma((mesh_size - 1,))
        return call(exchange_kernel, "exchange", (packed,), [vmem], scratch=[sems, sems], collective=collective)(
            outgoing
        )[0]

    all_rotations = shape((band_size, *rotation_rows.shape), bf16)
    zero, ghosts, rotations = call(
        turn_kernel,
        "turn",
        (rows, packed, all_rotations),
        [smem, smem, vmem, vmem],
        scratch=[
            pltpu.VMEM((nodes, count), f32),
            pltpu.VMEM((slots, count), f32),
            pltpu.VMEM((mesh_size, slots, count), bf16),
            *[dma((mesh_size - 1,))] * 2,
            *[dma((band_size - 1,))] * 2,
        ],
        collective=0,
    )(neighbour_ids, lists, filter_block, rotation_rows)
    one, outgoing = call(
        first_kernel,
        "first",
        (rows, packed),
        [smem] * 4 + [vmem] * 4,
        scratch=[table(extent), table(slots), *working],
        traffic=traffic,
    )(cell_map, cell_scale, neighbour_ids, lists, kernel, pot, zero, ghosts)
    all_pieces = shape((band_size, count, width), bf16)
    filtered, pieces, energy = call(
        second_kernel,
        "second",
        (shape((count, nodes), bf16), all_pieces, shape((8, count), f32)),
        [smem] * 2 + [vmem] * 5,
        scratch=[table(extent), *working],
        traffic=traffic,
    )(cell_map, cell_scale, kernel, pot, one, exchange(outgoing, 1), filter_block)
    pieces, energy = call(
        swap_kernel,
        "swap",
        (all_pieces, shape((mesh_size, 8, count), f32)),
        [anywhere, vmem],
        out_specs=(anywhere, vmem),
        scratch=[dma(()), *[dma((band_size - 1,))] * 2, *[dma((mesh_size - 1,))] * 2],
        collective=2,
    )(pieces, energy)
    rotated, energy = call(
        functools.partial(rotate_kernel, nodes * mesh_size, block),
        "rotate",
        (shape((rotation_rows.shape[1], width), bf16), shape((1, count), f32)),
        [smem, vmem, vmem, vmem],
    )(panel_owner, rotations, pieces, energy)
    return (filtered, rotated, energy[0])


def solution(mesh):
    placed = (
        P("band", "mesh"),
        P("mesh"),
        P("mesh"),
        P(),
        P(None, "mesh"),
        P("mesh", None),
        P("mesh", None, None),
        P("band", None),
        P(),
    )
    return jax.shard_map(
        per_device,
        mesh=mesh,
        in_specs=placed,
        out_specs=(P("band", "mesh"), P(None, ("mesh", "band")), P("band")),
        check_vma=False,
    )
```
